128 devices in a mesh: dp: 16 (over x_lo, z, core), expert: 8 (over x_hi, y).
Axes of the slice: x: 4 (x_hi: 2, x_lo: 2; x = x_hi * 2 + x_lo), y: 4, z: 4, core: 2. Of those that a mesh axis runs over, the one named last changes fastest.
Arguments:
- tokens: bfloat16 [2048, 3072], P(('dp', 'expert')), may hold values from -6 to 6
- router_weight: bfloat16 [8, 3072], replicated, may hold values from -0.109375 to 0.109375
- expert_ids: int32 [2048, 2], P(('dp', 'expert')), may hold values from 0 to 7, all different within a row; in each aligned block of 16 rows (0 to 15, 16 to 31, ...) at most 8 rows name the same one
- w_gate: bfloat16 [8, 3072, 8192], P('expert', None, 'dp'), may hold values from -0.109375 to 0.109375
- w_up: bfloat16 [8, 3072, 8192], P('expert', None, 'dp'), may hold values from -0.109375 to 0.109375
- w_down: bfloat16 [8, 8192, 3072], P('expert', 'dp'), may hold values from -0.0625 to 0.0625
- grad_out: bfloat16 [2048, 3072], P(('dp', 'expert')), may hold values from -6 to 6
Outputs:
- mixed: bfloat16 [2048, 3072], P(('dp', 'expert'))
- grad_tokens: bfloat16 [2048, 3072], P(('dp', 'expert'))
- grad_router: float32 [8, 3072], replicated
- grad_gate: bfloat16 [8, 3072, 8192], P('expert', None, 'dp')
- grad_up: bfloat16 [8, 3072, 8192], P('expert', None, 'dp')
- grad_down: bfloat16 [8, 8192, 3072], P('expert', 'dp')
The draws below stay inside these ranges and needn't reach their ends.
Inputs may be any that keep to these rules, and one draw needn't show every extreme that they name: `expert_ids`: the two experts of a token differ; among the rows of one device no expert is named more than 8 times; every expert is named by some row.
All inputs are finite; a program needn't handle non-finite values.
Results may differ from the reference program's by a relative error of at most 0.024.
Values may be sent and summed in bfloat16 or wider, within the bound.
No kernel may reach another device: no remote copies, remote signals or barrier semaphores. Data moves between devices by JAX's collectives and lax.ppermute only.
A program may use at most 128 MiB of HBM per device.

```python
import math
from functools import partial
import jax
import jax.numpy as jnp
import numpy as np
from jax import lax

D = 3072
FF = 8192
EXPERTS = 8
TOK_DEV = 16
CAP = 8
TOKENS = 2048
N_DP = 16


def steps_of(own_key, extent, shards, least, top_value):
    factor_of = 1.0
    for position, shards_of in shards:
        heights = jax.random.uniform(jax.random.fold_in(jax.random.fold_in(own_key, 6), position), (shards_of,), jnp.float32, least / len(shards), top_value / len(shards))
        factor_of = factor_of * jnp.repeat(jnp.exp(heights), extent[position] // shards_of).reshape((-1,) + (1,) * (len(extent) - 1 - position))
    return factor_of


def deal_out(stream_key, own, number, rows, number_of, top, most, lean):
    order = jax.random.permutation(stream_key, number_of)
    packed, usual = portions_of(number_of, rows * top, most, lean, True), portions_of(number_of, rows * top, most, lean, False)
    places = jnp.arange(number_of)

    def named(sizes, turn):
        used = int((sizes > 0).sum())
        fixed = max(1, used // 4)
        moved = fixed + (places - fixed + turn * (used - fixed)) % max(1, number_of - fixed)
        return jnp.zeros((number_of,), jnp.int32).at[order[jnp.where(places < fixed, places, moved)]].set(jnp.asarray(sizes, jnp.int32))

    sizes = jnp.where(number % 4 == 0, named(packed, number // 4), named(usual, number - number // 4 - 1))
    mixed = jax.random.permutation(jax.random.fold_in(own, 3), number_of)
    giver, taker = mixed[0:number_of // 2 * 2:2], mixed[1:number_of // 2 * 2:2]
    room = jnp.minimum(sizes[giver] - 1, most - sizes[taker]) // 2
    room = jnp.where((giver == order[0]) | (taker == order[0]) | (sizes[taker] == 0), 0, jnp.maximum(room, 0))
    moved = jax.random.randint(jax.random.fold_in(own, 4), (number_of // 2,), 0, 1 << 20) % (room + 1)
    sizes = sizes.at[giver].add(-moved).at[taker].add(moved)
    labels = jnp.searchsorted(jnp.cumsum(sizes), jnp.arange(rows * top), side="right").astype(jnp.int32)
    grid = labels.reshape(top, rows).T
    grid = grid[jax.random.permutation(jax.random.fold_in(own, 1), rows)]
    turn = jax.random.randint(jax.random.fold_in(own, 2), (rows, 1), 0, top)
    return jnp.take_along_axis(grid, (jnp.arange(top)[None, :] + turn) % top, axis=1)


def portions_of(count, total, limit, lean, full):
    portions = [(1 << 20) // math.isqrt(standing ** lean) + 1 for standing in range(1, count + 1)]
    largest = limit if full else min(limit, max(-(-total // count), total * portions[0] // sum(portions)))
    least = 1 if total - largest >= count - 1 else 0
    holding, spare = [largest] + [least] * (count - 1), total - largest - least * (count - 1)
    while spare > 0:
        free = [i for i in range(1, count) if holding[i] < largest] or [i for i in range(1, count) if holding[i] < limit]
        pool, remaining = sum([portions[i] for i in free]), spare
        for i in free:
            extra = min(limit - holding[i], max(1, remaining * portions[i] // pool), spare)
            holding[i] = holding[i] + extra
            spare = spare - extra
    return np.array(holding)


def scatter_about(rng, extent, deviation, bound, cuts=(), kind=jnp.bfloat16):
    entries = deviation * jax.random.normal(rng, extent, jnp.float32)
    if cuts:
        entries = entries * steps_of(rng, extent, cuts, -0.22, 0.18)
    return jnp.clip(entries, -bound, bound).astype(kind)


def setup_inputs(seed: int = 0) -> dict:
    key_of = jax.random.split(jax.random.key(seed), 8)
    tokens = scatter_about(key_of[0], (TOKENS, D), 1.0, 6.0, ((0, 128),))
    router_weight = scatter_about(key_of[1], (EXPERTS, D), D ** -0.5, 0.109375)
    expert_ids_keys = jax.random.split(jax.random.fold_in(key_of[2], 1), TOKENS // TOK_DEV)
    expert_ids_turns = jax.random.permutation(jax.random.fold_in(key_of[2], 3), TOKENS // TOK_DEV)
    expert_ids = jax.vmap(lambda own, number: deal_out(jax.random.fold_in(key_of[2], 2), own, number, TOK_DEV, EXPERTS, 2, CAP, 2))(expert_ids_keys, expert_ids_turns).reshape((TOKENS, 2))
    w_gate = scatter_about(key_of[3], (EXPERTS, D, FF), D ** -0.5, 0.109375, ((0, 8), (2, 16)))
    w_up = scatter_about(key_of[4], (EXPERTS, D, FF), D ** -0.5, 0.109375, ((0, 8), (2, 16)))
    w_down = scatter_about(key_of[5], (EXPERTS, FF, D), FF ** -0.5, 0.0625, ((0, 8), (1, 16)))
    grad_out = scatter_about(key_of[6], (TOKENS, D), 1.0, 6.0, ((0, 128),))
    return {"tokens": tokens, "router_weight": router_weight, "expert_ids": expert_ids, "w_gate": w_gate, "w_up": w_up, "w_down": w_down, "grad_out": grad_out}


HIGHEST = lax.Precision.HIGHEST


def dispatch_table(route_ids, experts, capacity):
    flat_ids = route_ids.reshape(-1)
    expert_range = jnp.arange(experts, dtype=jnp.int32)
    onehot = (flat_ids[:, None] == expert_range[None, :]).astype(jnp.int32)
    slot_rank = jnp.cumsum(onehot, axis=0) - onehot
    slot_index = jnp.sum(slot_rank * onehot, axis=1)
    target = flat_ids * capacity + slot_index
    column = jnp.arange(experts * capacity, dtype=jnp.int32)
    return (column[:, None] == target[None, :]).astype(jnp.float32)


def bf16_sum(terms):
    rounded = lax.optimization_barrier(terms.astype(jnp.bfloat16))
    return jnp.sum(rounded.astype(jnp.float32), axis=0).astype(jnp.bfloat16)


def one_expert(expert_items):
    row_block, grad_block, gate_matrix, up_matrix, down_matrix = expert_items
    row_total = row_block.shape[0]
    unit_count = FF // N_DP
    pre_gate = jnp.dot(row_block, gate_matrix, preferred_element_type=jnp.float32)
    pre_up = jnp.dot(row_block, up_matrix, preferred_element_type=jnp.float32)
    gate_sigmoid = jax.nn.sigmoid(pre_gate)
    gate_silu = pre_gate * gate_sigmoid
    hidden = (gate_silu * pre_up).astype(jnp.bfloat16)
    hidden_blocks = hidden.reshape(row_total, N_DP, unit_count).astype(jnp.float32)
    down_blocks = down_matrix.reshape(N_DP, unit_count, D).astype(jnp.float32)
    partial_out = jnp.einsum("rjf,jfd->jrd", hidden_blocks, down_blocks, precision=HIGHEST)
    expert_out = bf16_sum(partial_out)
    hidden_grad = lax.dot_general(grad_block, down_matrix, (((1,), (1,)), ((), ())), preferred_element_type=jnp.float32)
    silu_slope = gate_sigmoid * (1.0 + pre_gate * (1.0 - gate_sigmoid))
    up_grad = (hidden_grad * gate_silu).astype(jnp.bfloat16)
    gate_grad = (hidden_grad * pre_up * silu_slope).astype(jnp.bfloat16)
    down_total = lax.dot_general(hidden, grad_block, (((0,), (0,)), ((), ())), preferred_element_type=jnp.float32)
    gate_total = lax.dot_general(row_block, gate_grad, (((0,), (0,)), ((), ())), preferred_element_type=jnp.float32)
    up_total = lax.dot_general(row_block, up_grad, (((0,), (0,)), ((), ())), preferred_element_type=jnp.float32)
    gate_grad_blocks = gate_grad.reshape(row_total, N_DP, unit_count).astype(jnp.float32)
    up_grad_blocks = up_grad.reshape(row_total, N_DP, unit_count).astype(jnp.float32)
    gate_blocks = gate_matrix.reshape(D, N_DP, unit_count).astype(jnp.float32)
    up_blocks = up_matrix.reshape(D, N_DP, unit_count).astype(jnp.float32)
    back_partial = jnp.einsum("rjf,djf->jrd", gate_grad_blocks, gate_blocks, precision=HIGHEST)
    back_partial = back_partial + jnp.einsum("rjf,djf->jrd", up_grad_blocks, up_blocks, precision=HIGHEST)
    back_rows = bf16_sum(back_partial)
    return (expert_out, back_rows, gate_total.astype(jnp.bfloat16), up_total.astype(jnp.bfloat16),
            down_total.astype(jnp.bfloat16))


def reference(tokens, router_weight, expert_ids, w_gate, w_up, w_down, grad_out):
    experts = EXPERTS
    blocks = TOKENS // TOK_DEV
    logits = jnp.dot(tokens, router_weight.T, preferred_element_type=jnp.float32)
    expert_range = jnp.arange(experts, dtype=jnp.int32)
    first_hot = (expert_ids[:, 0:1] == expert_range[None, :]).astype(jnp.float32)
    second_hot = (expert_ids[:, 1:2] == expert_range[None, :]).astype(jnp.float32)
    first_logit = jnp.sum(logits * first_hot, axis=1)
    second_logit = jnp.sum(logits * second_hot, axis=1)
    share_first = jax.nn.sigmoid(first_logit - second_logit)
    share_second = jax.nn.sigmoid(second_logit - first_logit)
    tables = jax.vmap(partial(dispatch_table, experts=experts, capacity=CAP))(
        expert_ids.reshape(blocks, TOK_DEV, 2))
    token_tables = tables.reshape(blocks, experts * CAP, TOK_DEV, 2).sum(axis=3)
    token_blocks = tokens.reshape(blocks, TOK_DEV, D).astype(jnp.float32)
    placed = jnp.einsum("bst,btd->bsd", token_tables, token_blocks, precision=HIGHEST).astype(jnp.bfloat16)
    placed = placed.reshape(blocks, experts, CAP, D)
    expert_rows = jnp.transpose(placed, (1, 0, 2, 3)).reshape(experts, blocks * CAP, D)
    cotangent = grad_out.astype(jnp.float32)
    weighted = jnp.stack([share_first[:, None] * cotangent, share_second[:, None] * cotangent], axis=1)
    weighted = weighted.astype(jnp.bfloat16).reshape(blocks, 2 * TOK_DEV, D).astype(jnp.float32)
    placed_grads = jnp.einsum("bsa,bad->bsd", tables, weighted, precision=HIGHEST).astype(jnp.bfloat16)
    placed_grads = placed_grads.reshape(blocks, experts, CAP, D)
    grad_rows = jnp.transpose(placed_grads, (1, 0, 2, 3)).reshape(experts, blocks * CAP, D)
    expert_out, back_rows, grad_gate, grad_up, grad_down = lax.map(
        one_expert, (expert_rows, grad_rows, w_gate, w_up, w_down))
    out_blocks = jnp.transpose(expert_out.reshape(experts, blocks, CAP, D), (1, 0, 2, 3))
    out_blocks = out_blocks.reshape(blocks, experts * CAP, D).astype(jnp.float32)
    per_out = jnp.einsum("bsa,bsd->bad", tables, out_blocks, precision=HIGHEST).reshape(TOKENS, 2, D)
    mixed = (share_first[:, None] * per_out[:, 0] + share_second[:, None] * per_out[:, 1]).astype(jnp.bfloat16)
    back_blocks = jnp.transpose(back_rows.reshape(experts, blocks, CAP, D), (1, 0, 2, 3))
    back_blocks = back_blocks.reshape(blocks, experts * CAP, D).astype(jnp.float32)
    per_back = jnp.einsum("bsa,bsd->bad", tables, back_blocks, precision=HIGHEST).reshape(TOKENS, 2, D)
    dshare_first = jnp.sum(cotangent * per_out[:, 0], axis=1)
    dshare_second = jnp.sum(cotangent * per_out[:, 1], axis=1)
    logit_step = (dshare_first - dshare_second) * share_first * share_second
    logit_grad = logit_step[:, None] * (first_hot - second_hot)
    router_back = jnp.dot(logit_grad, router_weight.astype(jnp.float32), precision=HIGHEST)
    grad_tokens = (per_back[:, 0] + per_back[:, 1] + router_back).astype(jnp.bfloat16)
    grad_router = jnp.dot(logit_grad.T, tokens.astype(jnp.float32), precision=HIGHEST)
    return mixed, grad_tokens, grad_router, grad_gate, grad_up, grad_down
```

```python
import jax
import jax.numpy as jnp
from jax import lax
from jax.sharding import Mesh, PartitionSpec as P

CAP = 8
HIGHEST = lax.Precision.HIGHEST
BF16 = jnp.bfloat16
F32 = jnp.float32

AXES = ("xl", "z", "c", "xh", "y")
CHIPS = ("xl", "z")
OWNERS = ("xh", "y")
SHIFTS = [(dx, dz) for dx in range(2) for dz in range(4)]


def shift_perm(dx, dz):
    return [(a * 4 + b, ((a + dx) % 2) * 4 + (b + dz) % 4) for a in range(2) for b in range(4)]


def flip_perm(size, bit):
    return [(k, k ^ bit) for k in range(size)]


def dispatch_table(route_ids, experts, capacity):
    flat_ids = route_ids.reshape(-1)
    count = flat_ids.shape[0]
    place = jnp.arange(count, dtype=jnp.int32)
    same = (flat_ids[:, None] == flat_ids[None, :]) & (place[None, :] < place[:, None])
    slot_index = jnp.sum(same.astype(jnp.int32), axis=1)
    target = flat_ids * capacity + slot_index
    column = jnp.arange(experts * capacity, dtype=jnp.int32)
    return (column[:, None] == target[None, :]).astype(F32)


def contract_rows(left_side, right_side):
    return lax.dot_general(
        left_side, right_side, (((0,), (0,)), ((), ())), preferred_element_type=F32
    )


def contract_cols(left_side, right_side):
    return lax.dot_general(
        left_side, right_side, (((1,), (1,)), ((), ())), preferred_element_type=F32
    )


def swap_cores(rows):
    return lax.ppermute(rows, "c", [(0, 1), (1, 0)])


def gather_rows(own):
    blocks = [own]
    for dx, dz in SHIFTS[1:]:
        blocks.append(lax.ppermute(own, CHIPS, shift_perm(dx, dz)))
    mine = jnp.concatenate(blocks, axis=0)
    return jnp.concatenate([mine, swap_cores(mine)], axis=0)


def scatter_sum(merged, rows):
    total = merged[:rows].astype(F32)
    for n, (dx, dz) in enumerate(SHIFTS):
        if n:
            got = lax.ppermute(
                merged[n * rows : (n + 1) * rows], CHIPS, shift_perm(-dx % 2, -dz % 4)
            )
            total = total + got.astype(F32)
    return total.astype(BF16)


def all_sum(part):
    for axis, size, bit in (
        ("c", 2, 1),
        ("z", 4, 1),
        ("z", 4, 2),
        ("y", 4, 1),
        ("y", 4, 2),
        ("xl", 2, 1),
        ("xh", 2, 1),
    ):
        part = part + lax.ppermute(part, axis, flip_perm(size, bit))
    return part


def exchange(rows, experts, width):
    return lax.all_to_all(
        rows.reshape(experts, CAP, width), OWNERS, split_axis=0, concat_axis=0, tiled=True
    ).reshape(experts * CAP, width)


def on_device(tokens, router_weight, expert_ids, w_gate, w_up, w_down, grad_out):
    tok_count, model_width = tokens.shape
    experts = router_weight.shape[0]
    slot_count = experts * CAP
    half = 8 * slot_count
    slot_table = dispatch_table(expert_ids, experts, CAP)
    table_half = slot_table.astype(BF16)
    token_table = slot_table.reshape(slot_count, tok_count, 2).sum(axis=2).astype(BF16)
    placed = jnp.dot(token_table, tokens, preferred_element_type=F32).astype(BF16)
    arrived = exchange(placed, experts, model_width)

    logits = contract_cols(tokens, router_weight)
    expert_range = jnp.arange(experts, dtype=jnp.int32)
    first_hot = (expert_ids[:, 0:1] == expert_range[None, :]).astype(F32)
    second_hot = (expert_ids[:, 1:2] == expert_range[None, :]).astype(F32)
    first_logit = jnp.sum(logits * first_hot, axis=1)
    second_logit = jnp.sum(logits * second_hot, axis=1)
    share_first = jax.nn.sigmoid(first_logit - second_logit)
    share_second = jax.nn.sigmoid(second_logit - first_logit)
    cotangent = grad_out.astype(F32)
    weighted = jnp.stack(
        [share_first[:, None] * cotangent, share_second[:, None] * cotangent], axis=1
    )
    weighted = weighted.astype(BF16).reshape(2 * tok_count, model_width)
    placed_grads = jnp.dot(table_half, weighted, preferred_element_type=F32).astype(BF16)
    grad_arrived = exchange(placed_grads, experts, model_width)

    gathered = gather_rows(arrived)
    grad_gathered = gather_rows(grad_arrived)

    gate_matrix = w_gate[0]
    up_matrix = w_up[0]
    down_matrix = w_down[0]
    pre_gate = jnp.dot(gathered, gate_matrix, preferred_element_type=F32)
    pre_up = jnp.dot(gathered, up_matrix, preferred_element_type=F32)
    gate_sigmoid = jax.nn.sigmoid(pre_gate)
    gate_silu = pre_gate * gate_sigmoid
    hidden = (gate_silu * pre_up).astype(BF16)
    out_other = swap_cores(
        jnp.dot(hidden[half:], down_matrix, preferred_element_type=F32).astype(BF16)
    )
    out_mine = jnp.dot(hidden[:half], down_matrix, preferred_element_type=F32)
    out_rows = scatter_sum((out_mine + out_other.astype(F32)).astype(BF16), slot_count)
    returned = exchange(out_rows, experts, model_width)
    per_out = contract_rows(table_half, returned).reshape(tok_count, 2, model_width)
    mixed = (share_first[:, None] * per_out[:, 0] + share_second[:, None] * per_out[:, 1]).astype(
        BF16
    )

    hidden_grad = contract_cols(grad_gathered, down_matrix)
    silu_slope = gate_sigmoid * (1.0 + pre_gate * (1.0 - gate_sigmoid))
    up_grad = (hidden_grad * gate_silu).astype(BF16)
    gate_grad = (hidden_grad * pre_up * silu_slope).astype(BF16)

    def back(rows):
        return contract_cols(gate_grad[rows], gate_matrix) + contract_cols(
            up_grad[rows], up_matrix
        )

    back_other = swap_cores(back(slice(half, None)).astype(BF16))
    back_mine = back(slice(0, half))
    back_rows = scatter_sum((back_mine + back_other.astype(F32)).astype(BF16), slot_count)
    grad_down = contract_rows(hidden, grad_gathered).astype(BF16)[None]
    grad_gate = contract_rows(gathered, gate_grad).astype(BF16)[None]
    grad_up = contract_rows(gathered, up_grad).astype(BF16)[None]
    back_home = exchange(back_rows, experts, model_width)
    per_back = contract_rows(table_half, back_home).reshape(tok_count, 2, model_width)
    dshare_first = jnp.sum(cotangent * per_out[:, 0], axis=1)
    dshare_second = jnp.sum(cotangent * per_out[:, 1], axis=1)
    logit_step = (dshare_first - dshare_second) * share_first * share_second
    logit_grad = logit_step[:, None] * (first_hot - second_hot)
    router_back = jnp.dot(logit_grad, router_weight.astype(F32), precision=HIGHEST)
    grad_tokens = (per_back[:, 0] + per_back[:, 1] + router_back).astype(BF16)
    local_router = lax.dot_general(
        logit_grad,
        tokens.astype(F32),
        (((0,), (0,)), ((), ())),
        precision=HIGHEST,
        preferred_element_type=F32,
    )
    grad_router = all_sum(local_router)
    return (mixed, grad_tokens, grad_router, grad_gate, grad_up, grad_down)


def solution(mesh):
    fine = Mesh(mesh.devices.reshape(2, 4, 2, 2, 4), AXES)
    dp = ("xl", "z", "c")
    rows = P(AXES, None)
    return jax.shard_map(
        on_device,
        mesh=fine,
        in_specs=(
            rows,
            P(),
            rows,
            P(OWNERS, None, dp),
            P(OWNERS, None, dp),
            P(OWNERS, dp, None),
            rows,
        ),
        out_specs=(
            rows,
            rows,
            P(),
            P(OWNERS, None, dp),
            P(OWNERS, None, dp),
            P(OWNERS, dp, None),
        ),
        check_vma=False,
    )
```

```python
import jax
import jax.numpy as jnp
from jax import lax
from jax.sharding import Mesh, PartitionSpec as P

CAP = 8
HIGHEST = lax.Precision.HIGHEST
BF16 = jnp.bfloat16
F32 = jnp.float32

AXES = ("xl", "z", "c", "xh", "y")
CHIPS = ("xl", "z")
OWNERS = ("xh", "y")
EVERY = ("xl", "z", "xh", "y")


def flip_perm(size, bit):
    return [(k, k ^ bit) for k in range(size)]


def dispatch_table(route_ids, experts, capacity):
    flat_ids = route_ids.reshape(-1)
    count = flat_ids.shape[0]
    place = jnp.arange(count, dtype=jnp.int32)
    same = (flat_ids[:, None] == flat_ids[None, :]) & (place[None, :] < place[:, None])
    slot_index = jnp.sum(same.astype(jnp.int32), axis=1)
    target = flat_ids * capacity + slot_index
    column = jnp.arange(experts * capacity, dtype=jnp.int32)
    return (column[:, None] == target[None, :]).astype(F32)


def contract_rows(left_side, right_side):
    return lax.dot_general(
        left_side, right_side, (((0,), (0,)), ((), ())), preferred_element_type=F32
    )


def contract_cols(left_side, right_side):
    return lax.dot_general(
        left_side, right_side, (((1,), (1,)), ((), ())), preferred_element_type=F32
    )


def swap_cores(rows):
    return lax.ppermute(rows, "c", [(0, 1), (1, 0)])


def both_cores(mine):
    return jnp.concatenate([mine, swap_cores(mine)], axis=0)


def send_home(merged, experts, width):
    parts = lax.all_to_all(
        merged.reshape(8 * experts, CAP, width), EVERY, split_axis=0, concat_axis=0, tiled=True
    )
    total = parts.reshape(8, experts * CAP, width).astype(F32).sum(axis=0)
    return total.astype(BF16)


def all_sum(part):
    for axis, size, bit in (
        ("c", 2, 1),
        ("z", 4, 1),
        ("z", 4, 2),
        ("y", 4, 1),
        ("y", 4, 2),
        ("xl", 2, 1),
        ("xh", 2, 1),
    ):
        part = part + lax.ppermute(part, axis, flip_perm(size, bit))
    return part


def exchange(rows, experts, width):
    return lax.all_to_all(
        rows.reshape(experts, CAP, width), OWNERS, split_axis=0, concat_axis=0, tiled=True
    ).reshape(experts * CAP, width)


def on_device(tokens, router_weight, expert_ids, w_gate, w_up, w_down, grad_out):
    tok_count, model_width = tokens.shape
    experts = router_weight.shape[0]
    slot_count = experts * CAP
    half = 8 * slot_count
    slot_table = dispatch_table(expert_ids, experts, CAP)
    table_half = slot_table.astype(BF16)
    token_table = slot_table.reshape(slot_count, tok_count, 2).sum(axis=2).astype(BF16)
    placed = jnp.dot(
        jnp.tile(token_table, (8, 1)), tokens, preferred_element_type=F32
    ).astype(BF16)
    arrived = lax.all_to_all(
        placed.reshape(8 * experts, CAP, model_width),
        EVERY,
        split_axis=0,
        concat_axis=0,
        tiled=True,
    ).reshape(half, model_width)

    logits = contract_cols(tokens, router_weight)
    expert_range = jnp.arange(experts, dtype=jnp.int32)
    first_hot = (expert_ids[:, 0:1] == expert_range[None, :]).astype(F32)
    second_hot = (expert_ids[:, 1:2] == expert_range[None, :]).astype(F32)
    first_logit = jnp.sum(logits * first_hot, axis=1)
    second_logit = jnp.sum(logits * second_hot, axis=1)
    share_first = jax.nn.sigmoid(first_logit - second_logit)
    share_second = jax.nn.sigmoid(second_logit - first_logit)
    cotangent = grad_out.astype(F32)
    weighted = jnp.stack(
        [share_first[:, None] * cotangent, share_second[:, None] * cotangent], axis=1
    )
    weighted = weighted.astype(BF16).reshape(2 * tok_count, model_width)
    placed_grads = jnp.dot(table_half, weighted, preferred_element_type=F32).astype(BF16)
    grad_arrived = exchange(placed_grads, experts, model_width)

    gathered = both_cores(arrived)
    grad_gathered = both_cores(lax.all_gather(grad_arrived, CHIPS, axis=0, tiled=True))

    gate_matrix = w_gate[0]
    up_matrix = w_up[0]
    down_matrix = w_down[0]
    pre_gate = jnp.dot(gathered, gate_matrix, preferred_element_type=F32)
    pre_up = jnp.dot(gathered, up_matrix, preferred_element_type=F32)
    gate_sigmoid = jax.nn.sigmoid(pre_gate)
    gate_silu = pre_gate * gate_sigmoid
    after = grad_arrived[0, 0].astype(F32) * 0.0
    hidden = (gate_silu * pre_up + after).astype(BF16)
    out_other = swap_cores(
        jnp.dot(hidden[half:], down_matrix, preferred_element_type=F32).astype(BF16)
    )
    out_mine = jnp.dot(hidden[:half], down_matrix, preferred_element_type=F32)
    returned = send_home(
        (out_mine + out_other.astype(F32)).astype(BF16), experts, model_width
    )
    per_out = contract_rows(table_half, returned).reshape(tok_count, 2, model_width)
    mixed = (share_first[:, None] * per_out[:, 0] + share_second[:, None] * per_out[:, 1]).astype(
        BF16
    )

    hidden_grad = contract_cols(grad_gathered, down_matrix)
    silu_slope = gate_sigmoid * (1.0 + pre_gate * (1.0 - gate_sigmoid))
    up_grad = (hidden_grad * gate_silu).astype(BF16)
    gate_grad = (hidden_grad * pre_up * silu_slope).astype(BF16)

    def back(rows):
        return contract_cols(gate_grad[rows], gate_matrix) + contract_cols(
            up_grad[rows], up_matrix
        )

    back_other = swap_cores(back(slice(half, None)).astype(BF16))
    back_mine = back(slice(0, half))
    back_home = send_home(
        (back_mine + back_other.astype(F32)).astype(BF16), experts, model_width
    )
    grad_down = contract_rows(hidden, grad_gathered).astype(BF16)[None]
    grad_gate = contract_rows(gathered, gate_grad).astype(BF16)[None]
    grad_up = contract_rows(gathered, up_grad).astype(BF16)[None]
    per_back = contract_rows(table_half, back_home).reshape(tok_count, 2, model_width)
    dshare_first = jnp.sum(cotangent * per_out[:, 0], axis=1)
    dshare_second = jnp.sum(cotangent * per_out[:, 1], axis=1)
    logit_step = (dshare_first - dshare_second) * share_first * share_second
    logit_grad = logit_step[:, None] * (first_hot - second_hot)
    router_back = jnp.dot(logit_grad, router_weight.astype(F32), precision=HIGHEST)
    grad_tokens = (per_back[:, 0] + per_back[:, 1] + router_back).astype(BF16)
    local_router = lax.dot_general(
        logit_grad,
        tokens.astype(F32),
        (((0,), (0,)), ((), ())),
        precision=HIGHEST,
        preferred_element_type=F32,
    )
    grad_router = all_sum(local_router)
    return (mixed, grad_tokens, grad_router, grad_gate, grad_up, grad_down)


def solution(mesh):
    fine = Mesh(mesh.devices.reshape(2, 4, 2, 2, 4), AXES)
    dp = ("xl", "z", "c")
    rows = P(AXES, None)
    return jax.shard_map(
        on_device,
        mesh=fine,
        in_specs=(
            rows,
            P(),
            rows,
            P(OWNERS, None, dp),
            P(OWNERS, None, dp),
            P(OWNERS, dp, None),
            rows,
        ),
        out_specs=(
            rows,
            rows,
            P(),
            P(OWNERS, None, dp),
            P(OWNERS, None, dp),
            P(OWNERS, dp, None),
        ),
        check_vma=False,
    )
```

```python
import jax
import jax.numpy as jnp
from jax import lax
from jax.sharding import Mesh, PartitionSpec as P

CAP = 8
HIGHEST = lax.Precision.HIGHEST
BF16 = jnp.bfloat16
F32 = jnp.float32

AXES = ("xl", "z", "c", "xh", "y")
CHIPS = ("xl", "z")
OWNERS = ("xh", "y")
EVERY = ("xl", "z", "xh", "y")


def flip_perm(size, bit):
    return [(k, k ^ bit) for k in range(size)]


def slot_tables(route_ids, experts):
    count = route_ids.shape[0]
    place = jnp.arange(count, dtype=jnp.int32)
    earlier = place[None, :] < place[:, None]
    column = jnp.arange(experts * CAP, dtype=jnp.int32)
    tables = []
    for k in range(2):
        own = route_ids[:, k]
        rank = sum(
            jnp.sum((earlier & (own[:, None] == route_ids[:, m][None, :])).astype(jnp.int32), axis=1)
            for m in range(2)
        )
        tables.append((column[:, None] == (own * CAP + rank)[None, :]).astype(F32))
    return tables


def contract_rows(left_side, right_side):
    return lax.dot_general(
        left_side, right_side, (((0,), (0,)), ((), ())), preferred_element_type=F32
    )


def contract_cols(left_side, right_side):
    return lax.dot_general(
        left_side, right_side, (((1,), (1,)), ((), ())), preferred_element_type=F32
    )


def swap_cores(rows):
    return lax.ppermute(rows, "c", [(0, 1), (1, 0)])


def tie(value, *before):
    nothing = sum(b[(0,) * b.ndim].astype(F32) * 0.0 for b in before)
    return value + nothing.astype(value.dtype)


def spread(rows, experts, width):
    return lax.all_to_all(
        rows.reshape(8 * experts, CAP, width), EVERY, split_axis=0, concat_axis=0, tiled=True
    ).reshape(8 * experts * CAP, width)


def both_cores(mine):
    return jnp.concatenate([mine, swap_cores(mine)], axis=0)


def send_home(merged, experts, width):
    parts = lax.all_to_all(
        merged.reshape(8 * experts, CAP, width), EVERY, split_axis=0, concat_axis=0, tiled=True
    )
    total = parts.reshape(8, experts * CAP, width).astype(F32).sum(axis=0)
    return total.astype(BF16)


def all_sum(part):
    for axis, size, bit in (
        ("c", 2, 1),
        ("z", 4, 1),
        ("z", 4, 2),
        ("y", 4, 1),
        ("y", 4, 2),
        ("xl", 2, 1),
        ("xh", 2, 1),
    ):
        part = part + lax.ppermute(part, axis, flip_perm(size, bit))
    return part


def on_device(tokens, router_weight, expert_ids, w_gate, w_up, w_down, grad_out):
    tok_count, model_width = tokens.shape
    experts = router_weight.shape[0]
    slot_count = experts * CAP
    half = 8 * slot_count
    first_table, second_table = slot_tables(expert_ids, experts)
    token_table = jnp.tile((first_table + second_table).astype(BF16), (8, 1))
    placed = jnp.dot(
        token_table, tokens, preferred_element_type=F32
    ).astype(BF16)
    arrived = spread(placed, experts, model_width)

    logits = contract_cols(tokens, router_weight)
    expert_range = jnp.arange(experts, dtype=jnp.int32)
    first_hot = (expert_ids[:, 0:1] == expert_range[None, :]).astype(F32)
    second_hot = (expert_ids[:, 1:2] == expert_range[None, :]).astype(F32)
    first_logit = jnp.sum(logits * first_hot, axis=1)
    second_logit = jnp.sum(logits * second_hot, axis=1)
    share_first = jax.nn.sigmoid(first_logit - second_logit)
    share_second = jax.nn.sigmoid(second_logit - first_logit)
    cotangent = grad_out.astype(F32)
    slot_share = jnp.tile(
        jnp.sum(first_table * share_first + second_table * share_second, axis=1), 8
    )
    placed_grads = jnp.dot(token_table, grad_out, preferred_element_type=F32)
    placed_grads = (placed_grads * tie(slot_share, arrived)[:, None]).astype(BF16)
    grad_arrived = spread(placed_grads, experts, model_width)

    gathered = both_cores(arrived)

    gate_matrix = w_gate[0]
    up_matrix = w_up[0]
    down_matrix = w_down[0]
    pre_gate = jnp.dot(gathered, gate_matrix, preferred_element_type=F32)
    pre_up = jnp.dot(gathered, up_matrix, preferred_element_type=F32)
    gate_sigmoid = jax.nn.sigmoid(pre_gate)
    gate_silu = pre_gate * gate_sigmoid
    hidden = (gate_silu * pre_up).astype(BF16)
    out_other = swap_cores(
        jnp.dot(hidden[half:], down_matrix, preferred_element_type=F32).astype(BF16)
    )
    out_mine = jnp.dot(hidden[:half], down_matrix, preferred_element_type=F32)
    grad_gathered = both_cores(tie(grad_arrived, out_mine))
    returned = send_home(
        tie(out_mine + out_other.astype(F32), grad_arrived).astype(BF16), experts, model_width
    )

    hidden_grad = contract_cols(grad_gathered, down_matrix)
    silu_slope = gate_sigmoid * (1.0 + pre_gate * (1.0 - gate_sigmoid))
    up_grad = (hidden_grad * gate_silu).astype(BF16)
    gate_grad = (hidden_grad * pre_up * silu_slope).astype(BF16)

    def back(rows):
        return contract_cols(gate_grad[rows], gate_matrix) + contract_cols(
            up_grad[rows], up_matrix
        )

    back_other = swap_cores(back(slice(half, None)).astype(BF16))
    back_mine = back(slice(0, half))
    back_home = send_home(
        (back_mine + back_other.astype(F32)).astype(BF16), experts, model_width
    )
    grad_down = contract_rows(hidden, grad_gathered).astype(BF16)[None]
    grad_gate = contract_rows(gathered, gate_grad).astype(BF16)[None]
    grad_up = contract_rows(gathered, up_grad).astype(BF16)[None]
    home = tie(returned, grad_down, grad_gate, grad_up)
    first_out = contract_rows(first_table.astype(BF16), home)
    second_out = contract_rows(second_table.astype(BF16), home)
    mixed = (share_first[:, None] * first_out + share_second[:, None] * second_out).astype(
        BF16
    )
    both_back = contract_rows((first_table + second_table).astype(BF16), back_home)
    dshare_first = jnp.sum(cotangent * first_out, axis=1)
    dshare_second = jnp.sum(cotangent * second_out, axis=1)
    logit_step = (dshare_first - dshare_second) * share_first * share_second
    logit_grad = logit_step[:, None] * (first_hot - second_hot)
    router_back = jnp.dot(logit_grad, router_weight.astype(F32), precision=HIGHEST)
    grad_tokens = (both_back + router_back).astype(BF16)
    local_router = lax.dot_general(
        logit_grad,
        tokens.astype(F32),
        (((0,), (0,)), ((), ())),
        precision=HIGHEST,
        preferred_element_type=F32,
    )
    grad_router = all_sum(local_router)
    return (mixed, grad_tokens, grad_router, grad_gate, grad_up, grad_down)


def solution(mesh):
    fine = Mesh(mesh.devices.reshape(2, 4, 2, 2, 4), AXES)
    dp = ("xl", "z", "c")
    rows = P(AXES, None)
    return jax.shard_map(
        on_device,
        mesh=fine,
        in_specs=(
            rows,
            P(),
            rows,
            P(OWNERS, None, dp),
            P(OWNERS, None, dp),
            P(OWNERS, dp, None),
            rows,
        ),
        out_specs=(
            rows,
            rows,
            P(),
            P(OWNERS, None, dp),
            P(OWNERS, None, dp),
            P(OWNERS, dp, None),
        ),
        check_vma=False,
    )
```

```python
import jax
import jax.numpy as jnp
from jax import lax
from jax.sharding import Mesh, PartitionSpec as P

CAP = 8
HIGHEST = lax.Precision.HIGHEST
BF16 = jnp.bfloat16
F32 = jnp.float32

AXES = ("xl", "z", "c", "xh", "y")
CHIPS = ("xl", "z")
OWNERS = ("xh", "y")
HOLDERS = ("xl", "z", "c")
EVERY = ("xl", "z", "xh", "y")


def flip_perm(size, bit):
    return [(k, k ^ bit) for k in range(size)]


def slot_tables(route_ids, experts):
    count = route_ids.shape[0]
    place = jnp.arange(count, dtype=jnp.int32)
    earlier = place[None, :] < place[:, None]
    column = jnp.arange(experts * CAP, dtype=jnp.int32)
    tables = []
    for k in range(2):
        own = route_ids[:, k]
        rank = sum(
            jnp.sum((earlier & (own[:, None] == route_ids[:, m][None, :])).astype(jnp.int32), axis=1)
            for m in range(2)
        )
        tables.append((column[:, None] == (own * CAP + rank)[None, :]).astype(F32))
    return tables


def contract_rows(left_side, right_side):
    return lax.dot_general(
        left_side, right_side, (((0,), (0,)), ((), ())), preferred_element_type=F32
    )


def contract_cols(left_side, right_side):
    return lax.dot_general(
        left_side, right_side, (((1,), (1,)), ((), ())), preferred_element_type=F32
    )


def swap_cores(rows):
    return lax.ppermute(rows, "c", [(0, 1), (1, 0)])


def tie(value, *before):
    nothing = sum(b[(0,) * b.ndim].astype(F32) * 0.0 for b in before)
    return value + nothing.astype(value.dtype)


def exchange(rows, experts, width):
    return lax.all_to_all(
        rows.reshape(experts, CAP, width), OWNERS, split_axis=0, concat_axis=0, tiled=True
    ).reshape(experts * CAP, width)


def of_core(rows, core):
    blocks = rows.reshape(8, 2, -1, rows.shape[-1])
    picked = lax.dynamic_index_in_dim(blocks, core, axis=1, keepdims=False)
    return picked.reshape(-1, rows.shape[-1])


def send_home(merged, experts, width):
    parts = lax.all_to_all(
        merged.reshape(8 * experts, CAP, width), EVERY, split_axis=0, concat_axis=0, tiled=True
    )
    total = parts.reshape(8, experts * CAP, width).astype(F32).sum(axis=0)
    return total.astype(BF16)


def all_sum(part):
    for axis, size, bit in (
        ("c", 2, 1),
        ("z", 4, 1),
        ("z", 4, 2),
        ("y", 4, 1),
        ("y", 4, 2),
        ("xl", 2, 1),
        ("xh", 2, 1),
    ):
        part = part + lax.ppermute(part, axis, flip_perm(size, bit))
    return part


def on_device(tokens, router_weight, expert_ids, w_gate, w_up, w_down, grad_out):
    tok_count, model_width = tokens.shape
    experts = router_weight.shape[0]
    slot_count = experts * CAP
    first_table, second_table = slot_tables(expert_ids, experts)
    token_table = (first_table + second_table).astype(BF16)
    placed = jnp.dot(
        token_table, tokens, preferred_element_type=F32
    ).astype(BF16)
    arrived = exchange(placed, experts, model_width)

    logits = contract_cols(tokens, router_weight)
    expert_range = jnp.arange(experts, dtype=jnp.int32)
    first_hot = (expert_ids[:, 0:1] == expert_range[None, :]).astype(F32)
    second_hot = (expert_ids[:, 1:2] == expert_range[None, :]).astype(F32)
    first_logit = jnp.sum(logits * first_hot, axis=1)
    second_logit = jnp.sum(logits * second_hot, axis=1)
    share_first = jax.nn.sigmoid(first_logit - second_logit)
    share_second = jax.nn.sigmoid(second_logit - first_logit)
    cotangent = grad_out.astype(F32)
    slot_share = jnp.sum(first_table * share_first + second_table * share_second, axis=1)
    placed_grads = jnp.dot(token_table, grad_out, preferred_element_type=F32)
    placed_grads = (placed_grads * tie(slot_share, arrived)[:, None]).astype(BF16)
    grad_arrived = exchange(placed_grads, experts, model_width)

    gathered = lax.all_gather(arrived, HOLDERS, axis=0, tiled=True)
    grad_gathered = lax.all_gather(grad_arrived, HOLDERS, axis=0, tiled=True)
    core = lax.axis_index("c")

    gate_matrix = w_gate[0]
    up_matrix = w_up[0]
    down_matrix = w_down[0]
    pre_gate = jnp.dot(gathered, gate_matrix, preferred_element_type=F32)
    pre_up = jnp.dot(gathered, up_matrix, preferred_element_type=F32)
    gate_sigmoid = jax.nn.sigmoid(pre_gate)
    gate_silu = pre_gate * gate_sigmoid
    hidden = tie(gate_silu * pre_up, grad_arrived).astype(BF16)
    out_theirs = jnp.dot(
        of_core(hidden, 1 - core), down_matrix, preferred_element_type=F32
    ).astype(BF16)
    out_other = swap_cores(out_theirs)
    out_mine = jnp.dot(of_core(hidden, core), down_matrix, preferred_element_type=F32)
    out_merged = (out_mine + out_other.astype(F32)).astype(BF16)
    returned = send_home(out_merged, experts, model_width)
    hidden_grad = tie(contract_cols(grad_gathered, down_matrix), out_merged)
    silu_slope = gate_sigmoid * (1.0 + pre_gate * (1.0 - gate_sigmoid))
    up_grad = (hidden_grad * gate_silu).astype(BF16)
    gate_grad = (hidden_grad * pre_up * silu_slope).astype(BF16)

    def back(which):
        return contract_cols(of_core(gate_grad, which), gate_matrix) + contract_cols(
            of_core(up_grad, which), up_matrix
        )

    back_other = swap_cores(back(1 - core).astype(BF16))
    back_mine = back(core)
    grad_down = contract_rows(hidden, grad_gathered).astype(BF16)[None]
    grad_gate = contract_rows(gathered, gate_grad).astype(BF16)[None]
    grad_up = contract_rows(gathered, up_grad).astype(BF16)[None]
    back_home = send_home(
        tie(
            back_mine + back_other.astype(F32), returned, grad_down, grad_gate, grad_up
        ).astype(BF16), experts, model_width
    )
    home = returned
    first_out = contract_rows(first_table.astype(BF16), home)
    second_out = contract_rows(second_table.astype(BF16), home)
    mixed = (share_first[:, None] * first_out + share_second[:, None] * second_out).astype(
        BF16
    )
    both_back = contract_rows((first_table + second_table).astype(BF16), back_home)
    dshare_first = jnp.sum(cotangent * first_out, axis=1)
    dshare_second = jnp.sum(cotangent * second_out, axis=1)
    logit_step = (dshare_first - dshare_second) * share_first * share_second
    logit_grad = logit_step[:, None] * (first_hot - second_hot)
    router_back = jnp.dot(logit_grad, router_weight.astype(F32), precision=HIGHEST)
    grad_tokens = (both_back + router_back).astype(BF16)
    local_router = lax.dot_general(
        logit_grad,
        tokens.astype(F32),
        (((0,), (0,)), ((), ())),
        precision=HIGHEST,
        preferred_element_type=F32,
    )
    grad_router = all_sum(local_router)
    return (mixed, grad_tokens, grad_router, grad_gate, grad_up, grad_down)


def solution(mesh):
    fine = Mesh(mesh.devices.reshape(2, 4, 2, 2, 4), AXES)
    dp = ("xl", "z", "c")
    rows = P(AXES, None)
    return jax.shard_map(
        on_device,
        mesh=fine,
        in_specs=(
            rows,
            P(),
            rows,
            P(OWNERS, None, dp),
            P(OWNERS, None, dp),
            P(OWNERS, dp, None),
            rows,
        ),
        out_specs=(
            rows,
            rows,
            P(),
            P(OWNERS, None, dp),
            P(OWNERS, None, dp),
            P(OWNERS, dp, None),
        ),
        check_vma=False,
    )
```

```python
import jax
import jax.numpy as jnp
from jax import lax
from jax.sharding import Mesh, PartitionSpec as P

CAP = 8
HIGHEST = lax.Precision.HIGHEST
BF16 = jnp.bfloat16
F32 = jnp.float32

AXES = ("xl", "z", "c", "xh", "y")
CHIPS = ("xl", "z")
OWNERS = ("xh", "y")
HOLDERS = ("xl", "z", "c")
EVERY = ("xl", "z", "xh", "y")


def flip_perm(size, bit):
    return [(k, k ^ bit) for k in range(size)]


def slot_tables(route_ids, experts):
    count = route_ids.shape[0]
    place = jnp.arange(count, dtype=jnp.int32)
    earlier = place[None, :] < place[:, None]
    column = jnp.arange(experts * CAP, dtype=jnp.int32)
    tables = []
    for k in range(2):
        own = route_ids[:, k]
        rank = sum(
            jnp.sum((earlier & (own[:, None] == route_ids[:, m][None, :])).astype(jnp.int32), axis=1)
            for m in range(2)
        )
        tables.append((column[:, None] == (own * CAP + rank)[None, :]).astype(F32))
    return tables


def contract_rows(left_side, right_side):
    return lax.dot_general(
        left_side, right_side, (((0,), (0,)), ((), ())), preferred_element_type=F32
    )


def contract_cols(left_side, right_side):
    return lax.dot_general(
        left_side, right_side, (((1,), (1,)), ((), ())), preferred_element_type=F32
    )


def swap_cores(rows):
    return lax.ppermute(rows, "c", [(0, 1), (1, 0)])


def tie(value, *before):
    nothing = sum(b[(0,) * b.ndim].astype(F32) * 0.0 for b in before)
    return value + nothing.astype(value.dtype)


def exchange(rows, experts, width):
    return lax.all_to_all(
        rows.reshape(experts, CAP, width), OWNERS, split_axis=0, concat_axis=0, tiled=True
    ).reshape(experts * CAP, width)


def of_core(rows, core):
    blocks = rows.reshape(8, 2, -1, rows.shape[-1])
    picked = lax.dynamic_index_in_dim(blocks, core, axis=1, keepdims=False)
    return picked.reshape(-1, rows.shape[-1])


def send_home(merged, experts, width):
    parts = lax.all_to_all(
        merged.reshape(8 * experts, CAP, width), EVERY, split_axis=0, concat_axis=0, tiled=True
    )
    total = parts.reshape(8, experts * CAP, width).astype(F32).sum(axis=0)
    return total.astype(BF16)


def all_sum(part):
    part = part + lax.ppermute(part, "c", flip_perm(2, 1))
    for axis in ("z", "y", ("xl", "xh")):
        one, two, three = (lax.ppermute(part, axis, flip_perm(4, bit)) for bit in (1, 2, 3))
        part = (part + one) + (two + three)
    return part


def on_device(tokens, router_weight, expert_ids, w_gate, w_up, w_down, grad_out):
    tok_count, model_width = tokens.shape
    experts = router_weight.shape[0]
    slot_count = experts * CAP
    first_table, second_table = slot_tables(expert_ids, experts)
    token_table = (first_table + second_table).astype(BF16)
    placed = jnp.dot(
        token_table, tokens, preferred_element_type=F32
    ).astype(BF16)
    arrived = exchange(placed, experts, model_width)

    logits = contract_cols(tokens, router_weight)
    expert_range = jnp.arange(experts, dtype=jnp.int32)
    first_hot = (expert_ids[:, 0:1] == expert_range[None, :]).astype(F32)
    second_hot = (expert_ids[:, 1:2] == expert_range[None, :]).astype(F32)
    first_logit = jnp.sum(logits * first_hot, axis=1)
    second_logit = jnp.sum(logits * second_hot, axis=1)
    share_first = jax.nn.sigmoid(first_logit - second_logit)
    share_second = jax.nn.sigmoid(second_logit - first_logit)
    cotangent = grad_out.astype(F32)
    slot_share = jnp.sum(first_table * share_first + second_table * share_second, axis=1)
    placed_grads = jnp.dot(token_table, grad_out, preferred_element_type=F32)
    placed_grads = (placed_grads * tie(slot_share, arrived)[:, None]).astype(BF16)
    grad_arrived = exchange(placed_grads, experts, model_width)

    gathered = lax.all_gather(arrived, HOLDERS, axis=0, tiled=True)
    grad_gathered = lax.all_gather(grad_arrived, HOLDERS, axis=0, tiled=True)
    core = lax.axis_index("c")

    gate_matrix = w_gate[0]
    up_matrix = w_up[0]
    down_matrix = w_down[0]
    pre_gate = jnp.dot(gathered, gate_matrix, preferred_element_type=F32)
    pre_up = jnp.dot(gathered, up_matrix, preferred_element_type=F32)
    gate_sigmoid = jax.nn.sigmoid(pre_gate)
    gate_silu = pre_gate * gate_sigmoid
    hidden = tie(gate_silu * pre_up, grad_arrived).astype(BF16)
    out_theirs = jnp.dot(
        of_core(hidden, 1 - core), down_matrix, preferred_element_type=F32
    ).astype(BF16)
    out_other = swap_cores(out_theirs)
    out_mine = jnp.dot(of_core(hidden, core), down_matrix, preferred_element_type=F32)
    out_merged = (out_mine + out_other.astype(F32)).astype(BF16)
    returned = send_home(out_merged, experts, model_width)
    hidden_grad = tie(contract_cols(grad_gathered, down_matrix), out_merged)
    silu_slope = gate_sigmoid * (1.0 + pre_gate * (1.0 - gate_sigmoid))
    up_grad = (hidden_grad * gate_silu).astype(BF16)
    gate_grad = (hidden_grad * pre_up * silu_slope).astype(BF16)

    def back(which):
        return contract_cols(of_core(gate_grad, which), gate_matrix) + contract_cols(
            of_core(up_grad, which), up_matrix
        )

    back_other = swap_cores(back(1 - core).astype(BF16))
    back_mine = lax.optimization_barrier(back(core).astype(BF16))
    grad_down = contract_rows(hidden, grad_gathered).astype(BF16)[None]
    grad_gate = contract_rows(gathered, gate_grad).astype(BF16)[None]
    grad_up = contract_rows(gathered, up_grad).astype(BF16)[None]
    home = returned
    first_out = contract_rows(first_table.astype(BF16), home)
    second_out = contract_rows(second_table.astype(BF16), home)
    mixed = (share_first[:, None] * first_out + share_second[:, None] * second_out).astype(
        BF16
    )
    dshare_first = jnp.sum(cotangent * first_out, axis=1)
    dshare_second = jnp.sum(cotangent * second_out, axis=1)
    logit_step = (dshare_first - dshare_second) * share_first * share_second
    logit_grad = logit_step[:, None] * (first_hot - second_hot)
    router_back = jnp.dot(logit_grad, router_weight.astype(F32), precision=HIGHEST)
    local_router = lax.dot_general(
        logit_grad,
        tokens.astype(F32),
        (((0,), (0,)), ((), ())),
        precision=HIGHEST,
        preferred_element_type=F32,
    )
    grad_router = all_sum(local_router)
    back_home = send_home(
        tie(
            back_mine.astype(F32) + back_other.astype(F32), grad_router
        ).astype(BF16), experts, model_width
    )
    both_back = contract_rows((first_table + second_table).astype(BF16), back_home)
    grad_tokens = (both_back + router_back).astype(BF16)
    return (mixed, grad_tokens, grad_router, grad_gate, grad_up, grad_down)


def solution(mesh):
    fine = Mesh(mesh.devices.reshape(2, 4, 2, 2, 4), AXES)
    dp = ("xl", "z", "c")
    rows = P(AXES, None)
    return jax.shard_map(
        on_device,
        mesh=fine,
        in_specs=(
            rows,
            P(),
            rows,
            P(OWNERS, None, dp),
            P(OWNERS, None, dp),
            P(OWNERS, dp, None),
            rows,
        ),
        out_specs=(
            rows,
            rows,
            P(),
            P(OWNERS, None, dp),
            P(OWNERS, None, dp),
            P(OWNERS, dp, None),
        ),
        check_vma=False,
    )
```

```python
import jax
import jax.numpy as jnp
from jax import lax
from jax.sharding import Mesh, PartitionSpec as P

CAP = 8
HIGHEST = lax.Precision.HIGHEST
BF16 = jnp.bfloat16
F32 = jnp.float32

AXES = ("xl", "z", "c", "xh", "y")
CHIPS = ("xl", "z")
OWNERS = ("xh", "y")
HOLDERS = ("xl", "z", "c")
EVERY = ("xl", "z", "xh", "y")


def flip_perm(size, bit):
    return [(k, k ^ bit) for k in range(size)]


def slot_tables(route_ids, experts):
    count = route_ids.shape[0]
    place = jnp.arange(count, dtype=jnp.int32)
    earlier = place[None, :] < place[:, None]
    column = jnp.arange(experts * CAP, dtype=jnp.int32)
    tables = []
    for k in range(2):
        own = route_ids[:, k]
        rank = sum(
            jnp.sum((earlier & (own[:, None] == route_ids[:, m][None, :])).astype(jnp.int32), axis=1)
            for m in range(2)
        )
        tables.append((column[:, None] == (own * CAP + rank)[None, :]).astype(F32))
    return tables


def contract_rows(left_side, right_side):
    return lax.dot_general(
        left_side, right_side, (((0,), (0,)), ((), ())), preferred_element_type=F32
    )


def contract_cols(left_side, right_side):
    return lax.dot_general(
        left_side, right_side, (((1,), (1,)), ((), ())), preferred_element_type=F32
    )


def swap_cores(rows):
    return lax.ppermute(rows, "c", [(0, 1), (1, 0)])


def tie(value, *before):
    nothing = sum(b[(0,) * b.ndim].astype(F32) * 0.0 for b in before)
    return value + nothing.astype(value.dtype)


def exchange(rows, experts, width):
    return lax.all_to_all(
        rows.reshape(experts, CAP, width), OWNERS, split_axis=0, concat_axis=0, tiled=True
    ).reshape(experts * CAP, width)


def of_core(rows, core):
    blocks = rows.reshape(8, 2, -1, rows.shape[-1])
    picked = lax.dynamic_index_in_dim(blocks, core, axis=1, keepdims=False)
    return picked.reshape(-1, rows.shape[-1])


def send_home(merged, experts, width):
    parts = lax.all_to_all(
        merged.reshape(8 * experts, CAP, width), EVERY, split_axis=0, concat_axis=0, tiled=True
    )
    total = parts.reshape(8, experts * CAP, width).astype(F32).sum(axis=0)
    return total.astype(BF16)


def all_sum(part):
    for axis in ("z", "y", ("xl", "xh")):
        one, two, three = (lax.ppermute(part, axis, flip_perm(4, bit)) for bit in (1, 2, 3))
        part = (part + one) + (two + three)
    return part


def on_device(tokens, router_weight, expert_ids, w_gate, w_up, w_down, grad_out):
    tok_count, model_width = tokens.shape
    experts = router_weight.shape[0]
    slot_count = experts * CAP
    first_table, second_table = slot_tables(expert_ids, experts)
    token_table = (first_table + second_table).astype(BF16)
    placed = jnp.dot(
        token_table, tokens, preferred_element_type=F32
    ).astype(BF16)
    arrived = exchange(placed, experts, model_width)

    logits = contract_cols(tokens, router_weight)
    expert_range = jnp.arange(experts, dtype=jnp.int32)
    first_hot = (expert_ids[:, 0:1] == expert_range[None, :]).astype(F32)
    second_hot = (expert_ids[:, 1:2] == expert_range[None, :]).astype(F32)
    first_logit = jnp.sum(logits * first_hot, axis=1)
    second_logit = jnp.sum(logits * second_hot, axis=1)
    share_first = jax.nn.sigmoid(first_logit - second_logit)
    share_second = jax.nn.sigmoid(second_logit - first_logit)
    cotangent = grad_out.astype(F32)
    slot_share = jnp.sum(first_table * share_first + second_table * share_second, axis=1)
    placed_grads = jnp.dot(token_table, grad_out, preferred_element_type=F32)
    placed_grads = (placed_grads * tie(slot_share, arrived)[:, None]).astype(BF16)
    grad_arrived = exchange(placed_grads, experts, model_width)

    gathered = lax.all_gather(arrived, HOLDERS, axis=0, tiled=True)
    grad_gathered = lax.all_gather(grad_arrived, HOLDERS, axis=0, tiled=True)
    core = lax.axis_index("c")

    gate_matrix = w_gate[0]
    up_matrix = w_up[0]
    down_matrix = w_down[0]
    pre_gate = jnp.dot(gathered, gate_matrix, preferred_element_type=F32)
    pre_up = jnp.dot(gathered, up_matrix, preferred_element_type=F32)
    gate_sigmoid = jax.nn.sigmoid(pre_gate)
    gate_silu = pre_gate * gate_sigmoid
    hidden = tie(gate_silu * pre_up, grad_arrived).astype(BF16)
    out_theirs = jnp.dot(
        of_core(hidden, 1 - core), down_matrix, preferred_element_type=F32
    ).astype(BF16)
    out_other = swap_cores(out_theirs)
    out_mine = jnp.dot(of_core(hidden, core), down_matrix, preferred_element_type=F32)
    out_merged = (out_mine + out_other.astype(F32)).astype(BF16)
    returned = send_home(out_merged, experts, model_width)
    home = returned
    first_out = contract_rows(first_table.astype(BF16), home)
    second_out = contract_rows(second_table.astype(BF16), home)
    mixed = (share_first[:, None] * first_out + share_second[:, None] * second_out).astype(
        BF16
    )
    dshare_first = jnp.sum(cotangent * first_out, axis=1)
    dshare_second = jnp.sum(cotangent * second_out, axis=1)
    logit_step = (dshare_first - dshare_second) * share_first * share_second
    logit_grad = logit_step[:, None] * (first_hot - second_hot)
    router_back = jnp.dot(logit_grad, router_weight.astype(F32), precision=HIGHEST)
    local_router = lax.dot_general(
        logit_grad,
        tokens.astype(F32),
        (((0,), (0,)), ((), ())),
        precision=HIGHEST,
        preferred_element_type=F32,
    )
    local_router = local_router + swap_cores(local_router)
    hidden_grad = tie(contract_cols(grad_gathered, down_matrix), out_merged, local_router)
    silu_slope = gate_sigmoid * (1.0 + pre_gate * (1.0 - gate_sigmoid))
    up_grad = (hidden_grad * gate_silu).astype(BF16)
    gate_grad = (hidden_grad * pre_up * silu_slope).astype(BF16)

    def back(which):
        return contract_cols(of_core(gate_grad, which), gate_matrix) + contract_cols(
            of_core(up_grad, which), up_matrix
        )

    back_other = swap_cores(back(1 - core).astype(BF16))
    back_mine = lax.optimization_barrier(back(core).astype(BF16))
    grad_down = contract_rows(hidden, grad_gathered).astype(BF16)[None]
    grad_gate = contract_rows(gathered, gate_grad).astype(BF16)[None]
    grad_up = contract_rows(gathered, up_grad).astype(BF16)[None]
    grad_router = all_sum(local_router)
    back_home = send_home(
        tie(
            back_mine.astype(F32) + back_other.astype(F32), grad_router
        ).astype(BF16), experts, model_width
    )
    both_back = contract_rows((first_table + second_table).astype(BF16), back_home)
    grad_tokens = (both_back + router_back).astype(BF16)
    return (mixed, grad_tokens, grad_router, grad_gate, grad_up, grad_down)


def solution(mesh):
    fine = Mesh(mesh.devices.reshape(2, 4, 2, 2, 4), AXES)
    dp = ("xl", "z", "c")
    rows = P(AXES, None)
    return jax.shard_map(
        on_device,
        mesh=fine,
        in_specs=(
            rows,
            P(),
            rows,
            P(OWNERS, None, dp),
            P(OWNERS, None, dp),
            P(OWNERS, dp, None),
            rows,
        ),
        out_specs=(
            rows,
            rows,
            P(),
            P(OWNERS, None, dp),
            P(OWNERS, None, dp),
            P(OWNERS, dp, None),
        ),
        check_vma=False,
    )
```

```python
import jax
import jax.numpy as jnp
from jax import lax
from jax.sharding import Mesh, PartitionSpec as P

CAP = 8
HIGHEST = lax.Precision.HIGHEST
BF16 = jnp.bfloat16
F32 = jnp.float32

AXES = ("xl", "z", "c", "xh", "y")
CHIPS = ("xl", "z")
OWNERS = ("xh", "y")
HOLDERS = ("xl", "z", "c")
EVERY = ("xl", "z", "xh", "y")


def flip_perm(size, bit):
    return [(k, k ^ bit) for k in range(size)]


def slot_tables(route_ids, experts):
    count = route_ids.shape[0]
    place = jnp.arange(count, dtype=jnp.int32)
    earlier = place[None, :] < place[:, None]
    column = jnp.arange(experts * CAP, dtype=jnp.int32)
    tables = []
    for k in range(2):
        own = route_ids[:, k]
        rank = sum(
            jnp.sum((earlier & (own[:, None] == route_ids[:, m][None, :])).astype(jnp.int32), axis=1)
            for m in range(2)
        )
        tables.append((column[:, None] == (own * CAP + rank)[None, :]).astype(F32))
    return tables


def contract_rows(left_side, right_side):
    return lax.dot_general(
        left_side, right_side, (((0,), (0,)), ((), ())), preferred_element_type=F32
    )


def contract_cols(left_side, right_side):
    return lax.dot_general(
        left_side, right_side, (((1,), (1,)), ((), ())), preferred_element_type=F32
    )


def swap_cores(rows):
    return lax.ppermute(rows, "c", [(0, 1), (1, 0)])


def tie(value, *before):
    nothing = sum(b[(0,) * b.ndim].astype(F32) * 0.0 for b in before)
    return value + nothing.astype(value.dtype)


def exchange(rows, experts, width):
    return lax.all_to_all(
        rows.reshape(experts, CAP, width), OWNERS, split_axis=0, concat_axis=0, tiled=True
    ).reshape(experts * CAP, width)


def of_core(rows, core):
    blocks = rows.reshape(8, 2, -1, rows.shape[-1])
    picked = lax.dynamic_index_in_dim(blocks, core, axis=1, keepdims=False)
    return picked.reshape(-1, rows.shape[-1])


def send_home(merged, experts, width):
    parts = lax.all_to_all(
        merged.reshape(8 * experts, CAP, width), EVERY, split_axis=0, concat_axis=0, tiled=True
    )
    total = parts.reshape(8, experts * CAP, width).astype(F32).sum(axis=0)
    return total.astype(BF16)


def all_sum(part):
    for axis in ("z", "y", ("xl", "xh")):
        part = lax.reduce_precision(part, 8, 7)
        rounded = part.astype(BF16)
        one, two, three = (
            lax.ppermute(rounded, axis, flip_perm(4, bit)).astype(F32) for bit in (1, 2, 3)
        )
        part = (part + one) + (two + three)
    return part


def on_device(tokens, router_weight, expert_ids, w_gate, w_up, w_down, grad_out):
    tok_count, model_width = tokens.shape
    experts = router_weight.shape[0]
    slot_count = experts * CAP
    first_table, second_table = slot_tables(expert_ids, experts)
    token_table = (first_table + second_table).astype(BF16)
    placed = jnp.dot(
        token_table, tokens, preferred_element_type=F32
    ).astype(BF16)
    arrived = exchange(placed, experts, model_width)

    logits = contract_cols(tokens, router_weight)
    expert_range = jnp.arange(experts, dtype=jnp.int32)
    first_hot = (expert_ids[:, 0:1] == expert_range[None, :]).astype(F32)
    second_hot = (expert_ids[:, 1:2] == expert_range[None, :]).astype(F32)
    first_logit = jnp.sum(logits * first_hot, axis=1)
    second_logit = jnp.sum(logits * second_hot, axis=1)
    share_first = jax.nn.sigmoid(first_logit - second_logit)
    share_second = jax.nn.sigmoid(second_logit - first_logit)
    cotangent = grad_out.astype(F32)
    slot_share = jnp.sum(first_table * share_first + second_table * share_second, axis=1)
    placed_grads = jnp.dot(token_table, grad_out, preferred_element_type=F32)
    placed_grads = (placed_grads * tie(slot_share, arrived)[:, None]).astype(BF16)
    grad_arrived = exchange(placed_grads, experts, model_width)

    gathered = lax.all_gather(arrived, HOLDERS, axis=0, tiled=True)
    grad_gathered = lax.all_gather(grad_arrived, HOLDERS, axis=0, tiled=True)
    core = lax.axis_index("c")

    gate_matrix = w_gate[0]
    up_matrix = w_up[0]
    down_matrix = w_down[0]
    pre_gate = jnp.dot(gathered, gate_matrix, preferred_element_type=F32)
    pre_up = jnp.dot(gathered, up_matrix, preferred_element_type=F32)
    gate_sigmoid = jax.nn.sigmoid(pre_gate)
    gate_silu = pre_gate * gate_sigmoid
    hidden = tie(gate_silu * pre_up, grad_arrived).astype(BF16)
    out_theirs = jnp.dot(
        of_core(hidden, 1 - core), down_matrix, preferred_element_type=F32
    ).astype(BF16)
    out_other = swap_cores(out_theirs)
    out_mine = lax.optimization_barrier(
        jnp.dot(of_core(hidden, core), down_matrix, preferred_element_type=F32).astype(BF16)
    )
    out_merged = (out_mine.astype(F32) + out_other.astype(F32)).astype(BF16)
    returned = send_home(out_merged, experts, model_width)
    home = returned
    first_out = contract_rows(first_table.astype(BF16), home)
    second_out = contract_rows(second_table.astype(BF16), home)
    mixed = (share_first[:, None] * first_out + share_second[:, None] * second_out).astype(
        BF16
    )
    dshare_first = jnp.sum(cotangent * first_out, axis=1)
    dshare_second = jnp.sum(cotangent * second_out, axis=1)
    logit_step = (dshare_first - dshare_second) * share_first * share_second
    logit_grad = logit_step[:, None] * (first_hot - second_hot)
    router_back = jnp.dot(logit_grad, router_weight.astype(F32), precision=HIGHEST)
    local_router = lax.dot_general(
        logit_grad,
        tokens.astype(F32),
        (((0,), (0,)), ((), ())),
        precision=HIGHEST,
        preferred_element_type=F32,
    )
    local_router = local_router + swap_cores(local_router)
    hidden_grad = tie(contract_cols(grad_gathered, down_matrix), out_merged, local_router)
    silu_slope = gate_sigmoid * (1.0 + pre_gate * (1.0 - gate_sigmoid))
    up_grad = (hidden_grad * gate_silu).astype(BF16)
    gate_grad = (hidden_grad * pre_up * silu_slope).astype(BF16)

    def back(which):
        return contract_cols(of_core(gate_grad, which), gate_matrix) + contract_cols(
            of_core(up_grad, which), up_matrix
        )

    back_other = swap_cores(back(1 - core).astype(BF16))
    back_mine = lax.optimization_barrier(back(core).astype(BF16))
    grad_down = contract_rows(hidden, grad_gathered).astype(BF16)[None]
    grad_gate = contract_rows(gathered, gate_grad).astype(BF16)[None]
    grad_up = contract_rows(gathered, up_grad).astype(BF16)[None]
    grad_router = all_sum(local_router)
    back_home = send_home(
        tie(
            back_mine.astype(F32) + back_other.astype(F32), grad_router
        ).astype(BF16), experts, model_width
    )
    both_back = contract_rows((first_table + second_table).astype(BF16), back_home)
    grad_tokens = (both_back + router_back).astype(BF16)
    return (mixed, grad_tokens, grad_router, grad_gate, grad_up, grad_down)


def solution(mesh):
    fine = Mesh(mesh.devices.reshape(2, 4, 2, 2, 4), AXES)
    dp = ("xl", "z", "c")
    rows = P(AXES, None)
    return jax.shard_map(
        on_device,
        mesh=fine,
        in_specs=(
            rows,
            P(),
            rows,
            P(OWNERS, None, dp),
            P(OWNERS, None, dp),
            P(OWNERS, dp, None),
            rows,
        ),
        out_specs=(
            rows,
            rows,
            P(),
            P(OWNERS, None, dp),
            P(OWNERS, None, dp),
            P(OWNERS, dp, None),
        ),
        check_vma=False,
    )
```

```python
import jax
import jax.numpy as jnp
from jax import lax
from jax.sharding import Mesh, PartitionSpec as P

CAP = 8
HIGHEST = lax.Precision.HIGHEST
BF16 = jnp.bfloat16
F32 = jnp.float32

AXES = ("xl", "z", "c", "xh", "y")
CHIPS = ("xl", "z")
OWNERS = ("xh", "y")
HOLDERS = ("xl", "z", "c")
EVERY = ("xl", "z", "xh", "y")


def flip_perm(size, bit):
    return [(k, k ^ bit) for k in range(size)]


def slot_tables(route_ids, experts):
    count = route_ids.shape[0]
    place = jnp.arange(count, dtype=jnp.int32)
    earlier = place[None, :] < place[:, None]
    column = jnp.arange(experts * CAP, dtype=jnp.int32)
    tables = []
    for k in range(2):
        own = route_ids[:, k]
        rank = sum(
            jnp.sum((earlier & (own[:, None] == route_ids[:, m][None, :])).astype(jnp.int32), axis=1)
            for m in range(2)
        )
        tables.append((column[:, None] == (own * CAP + rank)[None, :]).astype(F32))
    return tables


def contract_rows(left_side, right_side):
    return lax.dot_general(
        left_side, right_side, (((0,), (0,)), ((), ())), preferred_element_type=F32
    )


def contract_cols(left_side, right_side):
    return lax.dot_general(
        left_side, right_side, (((1,), (1,)), ((), ())), preferred_element_type=F32
    )


def swap_cores(rows):
    return lax.ppermute(rows, "c", [(0, 1), (1, 0)])


def tie(value, *before):
    nothing = sum(b[(0,) * b.ndim].astype(F32) * 0.0 for b in before)
    return value + nothing.astype(value.dtype)


def exchange(rows, experts, width):
    return lax.all_to_all(
        rows.reshape(experts, CAP, width), OWNERS, split_axis=0, concat_axis=0, tiled=True
    ).reshape(experts * CAP, width)


def of_core(rows, core):
    blocks = rows.reshape(8, 2, -1, rows.shape[-1])
    picked = lax.dynamic_index_in_dim(blocks, core, axis=1, keepdims=False)
    return picked.reshape(-1, rows.shape[-1])


def send_home(merged, experts, width):
    parts = lax.all_to_all(
        merged.reshape(8 * experts, CAP, width), EVERY, split_axis=0, concat_axis=0, tiled=True
    )
    total = parts.reshape(8, experts * CAP, width).astype(F32).sum(axis=0)
    return total.astype(BF16)


def all_sum(part):
    for axis in ("z", "y", ("xl", "xh")):
        part = lax.reduce_precision(part, 8, 7)
        rounded = part.astype(BF16)
        one, two, three = (
            lax.ppermute(rounded, axis, flip_perm(4, bit)).astype(F32) for bit in (1, 2, 3)
        )
        part = (part + one) + (two + three)
    return part


def on_device(tokens, router_weight, expert_ids, w_gate, w_up, w_down, grad_out):
    tok_count, model_width = tokens.shape
    experts = router_weight.shape[0]
    slot_count = experts * CAP
    first_table, second_table = slot_tables(expert_ids, experts)
    token_table = (first_table + second_table).astype(BF16)
    placed = jnp.dot(
        token_table, tokens, preferred_element_type=F32
    ).astype(BF16)
    arrived = exchange(placed, experts, model_width)

    logits = contract_cols(tokens, router_weight)
    expert_range = jnp.arange(experts, dtype=jnp.int32)
    first_hot = (expert_ids[:, 0:1] == expert_range[None, :]).astype(F32)
    second_hot = (expert_ids[:, 1:2] == expert_range[None, :]).astype(F32)
    first_logit = jnp.sum(logits * first_hot, axis=1)
    second_logit = jnp.sum(logits * second_hot, axis=1)
    share_first = jax.nn.sigmoid(first_logit - second_logit)
    share_second = jax.nn.sigmoid(second_logit - first_logit)
    cotangent = grad_out.astype(F32)
    slot_share = jnp.sum(first_table * share_first + second_table * share_second, axis=1)
    placed_grads = jnp.dot(token_table, grad_out, preferred_element_type=F32)
    placed_grads = (placed_grads * tie(slot_share, arrived)[:, None]).astype(BF16)
    grad_arrived = exchange(placed_grads, experts, model_width)

    gathered = lax.all_gather(arrived, HOLDERS, axis=0, tiled=True)
    grad_gathered = lax.all_gather(grad_arrived, HOLDERS, axis=0, tiled=True)
    core = lax.axis_index("c")

    gate_matrix = w_gate[0]
    up_matrix = w_up[0]
    down_matrix = w_down[0]
    pre_gate = jnp.dot(gathered, gate_matrix, preferred_element_type=F32)
    pre_up = jnp.dot(gathered, up_matrix, preferred_element_type=F32)
    gate_sigmoid = jax.nn.sigmoid(pre_gate)
    gate_silu = pre_gate * gate_sigmoid
    hidden = tie(gate_silu * pre_up, grad_arrived).astype(BF16)
    out_theirs = jnp.dot(
        of_core(hidden, 1 - core), down_matrix, preferred_element_type=F32
    ).astype(BF16)
    out_other = swap_cores(out_theirs)
    out_mine = lax.optimization_barrier(
        jnp.dot(of_core(hidden, core), down_matrix, preferred_element_type=F32).astype(BF16)
    )
    out_merged = (out_mine.astype(F32) + out_other.astype(F32)).astype(BF16)
    returned = send_home(out_merged, experts, model_width)
    home = returned
    first_out = contract_rows(first_table.astype(BF16), home)
    second_out = contract_rows(second_table.astype(BF16), home)
    mixed = (share_first[:, None] * first_out + share_second[:, None] * second_out).astype(
        BF16
    )
    dshare_first = jnp.sum(cotangent * first_out, axis=1)
    dshare_second = jnp.sum(cotangent * second_out, axis=1)
    logit_step = (dshare_first - dshare_second) * share_first * share_second
    logit_grad = logit_step[:, None] * (first_hot - second_hot)
    router_back = jnp.dot(logit_grad, router_weight.astype(F32), precision=HIGHEST)
    local_router = lax.dot_general(
        logit_grad,
        tokens.astype(F32),
        (((0,), (0,)), ((), ())),
        precision=HIGHEST,
        preferred_element_type=F32,
    )
    local_router = local_router + swap_cores(local_router)
    hidden_grad = tie(contract_cols(grad_gathered, down_matrix), out_merged, local_router)
    silu_slope = gate_sigmoid * (1.0 + pre_gate * (1.0 - gate_sigmoid))
    up_grad = (hidden_grad * gate_silu).astype(BF16)
    gate_grad = (hidden_grad * pre_up * silu_slope).astype(BF16)

    def back(which):
        return contract_cols(of_core(up_grad, which), up_matrix) + contract_cols(
            of_core(gate_grad, which), gate_matrix
        )

    back_other = swap_cores(back(1 - core).astype(BF16))
    back_mine = lax.optimization_barrier(back(core).astype(BF16))
    grad_down = contract_rows(hidden, grad_gathered).astype(BF16)[None]
    grad_gate = contract_rows(gathered, gate_grad).astype(BF16)[None]
    grad_up = contract_rows(gathered, up_grad).astype(BF16)[None]
    grad_router = all_sum(local_router)
    back_home = send_home(
        tie(
            back_mine.astype(F32) + back_other.astype(F32), grad_router
        ).astype(BF16), experts, model_width
    )
    both_back = contract_rows((first_table + second_table).astype(BF16), back_home)
    grad_tokens = (both_back + router_back).astype(BF16)
    return (mixed, grad_tokens, grad_router, grad_gate, grad_up, grad_down)


def solution(mesh):
    fine = Mesh(mesh.devices.reshape(2, 4, 2, 2, 4), AXES)
    dp = ("xl", "z", "c")
    rows = P(AXES, None)
    return jax.shard_map(
        on_device,
        mesh=fine,
        in_specs=(
            rows,
            P(),
            rows,
            P(OWNERS, None, dp),
            P(OWNERS, None, dp),
            P(OWNERS, dp, None),
            rows,
        ),
        out_specs=(
            rows,
            rows,
            P(),
            P(OWNERS, None, dp),
            P(OWNERS, None, dp),
            P(OWNERS, dp, None),
        ),
        check_vma=False,
    )
```
